32 devices in a mesh: groups: 2 (over x), arc: 2 (over core), blk: 8 (over z, y).
Axes of the slice: x: 2, y: 2, z: 4, core: 2. Of those that a mesh axis runs over, the one named last changes fastest.
Arguments:
- queries: bfloat16 [6144, 640], P(('groups', 'arc', 'blk')), parts along dimension 0, may hold values from -128 to 128
- keys: bfloat16 [6144, 640], P(('groups', 'arc', 'blk')), parts along dimension 0, may hold values from -4 to 4
- values: bfloat16 [6144, 640], P(('groups', 'arc', 'blk')), parts along dimension 0, may hold values from -6 to 6
- out_weight: bfloat16 [640, 1024], replicated, may hold values from -0.25 to 0.25
- covis: int32 [192, 96], P('groups'), parts along dimension 0, may hold values from 0 to 1, as said below
- block_view: int32 [192], P('groups'), parts along dimension 0, may hold values from 0 to 95, each once
Outputs:
- projected: bfloat16 [6144, 1024], P(('groups', 'arc', 'blk')), parts along dimension 0
The draws below stay inside these ranges and needn't reach their ends.
There are 2 independent parts, one for each index of `groups`. The reference program is written for one: setup_inputs(seed, part) draws one part's arguments, and reference() takes and returns one part's arrays. A program takes and returns all parts, laid end to end along the dimension named above; an argument that names none is the same for every part. Nothing has to cross between parts.
Inputs may be any that keep to these rules, and one draw needn't show every extreme that they name: `covis`: symmetric, with ones on the diagonal. `block_view`: each view once.
All inputs are finite; a program needn't handle non-finite values.
Results may differ from the reference program's by a relative error of at most 0.008.
Values may be sent and summed in bfloat16 or wider, within the bound.
A program may use at most 128 MiB of HBM per device.

```python
import jax
import jax.numpy as jnp
from jax import lax

D = 1024
HEADS = 10
HD = 64
BLOCK = 32
TOKENS = 3072
NB = 96


def make_pair(key):
    base = jax.random.fold_in(key, 101)
    key_q, key_k = jax.random.split(base, 2)
    width = HEADS * HD
    query_part = jax.random.truncated_normal(key_q, -4.0, 4.0, (TOKENS, width), jnp.float32)
    key_part = jax.random.truncated_normal(key_k, -4.0, 4.0, (TOKENS, width), jnp.float32)
    query_part = 2.0 * query_part
    return (query_part, key_part)


def draw_queries(key, part):
    return make_pair(key)[0].astype(jnp.bfloat16)


def draw_keys(key, part):
    return make_pair(key)[1].astype(jnp.bfloat16)


def draw_covis(key, part):
    base = jax.random.fold_in(key, 202)
    key_a, key_b = jax.random.split(base, 2)
    raw = jax.random.randint(key_a, (NB, NB), 0, 16)
    paired = raw + raw.T
    index = jnp.arange(NB, dtype=jnp.int32)
    apart = jnp.abs(index[:, None] - index[None, :])
    apart = jnp.minimum(apart, NB - apart)
    reach = jax.random.randint(key_b, (NB,), 1, NB // 2 + 1)
    limit = jnp.maximum(reach[:, None], reach[None, :])
    linked = (apart <= limit) & (paired >= 8)
    linked = linked | (index[:, None] == index[None, :])
    return linked.astype(jnp.int32)


def block_scale(key, extent, cuts, low, high):
    def one(position, parts):
        steps = jax.random.uniform(jax.random.fold_in(jax.random.fold_in(key, 6), position), (parts,), jnp.float32, low / len(cuts), high / len(cuts))
        return jnp.repeat(jnp.exp(steps), extent[position] // parts).reshape((-1,) + (1,) * (len(extent) - position - 1))

    gain = one(*cuts[0])
    for cut in cuts[1:]:
        gain = gain * one(*cut)
    return gain


def scatter_about(own_key, extent, deviation, most, shards=(), kind=jnp.bfloat16):
    factor_of = block_scale(own_key, extent, shards, -0.22, 0.18) if shards else 1.0
    entries = jax.random.normal(own_key, extent, jnp.float32) * deviation * factor_of
    return jnp.minimum(jnp.maximum(entries, -most), most).astype(kind)


def setup_inputs(seed: int = 0, part: int = 0) -> dict:
    splits = jax.random.split(jax.random.key(seed), 7)
    own_keys = jax.random.split(jax.random.fold_in(splits[6], part), 7)
    return {
        "queries": draw_queries(jax.random.fold_in(jax.random.fold_in(splits[6], part), 71), part),
        "keys": draw_keys(jax.random.fold_in(jax.random.fold_in(splits[6], part), 71), part),
        "values": scatter_about(own_keys[2], (TOKENS, HEADS * HD), 1.0, 6.0, ((0, 16),)),
        "out_weight": scatter_about(splits[3], (HEADS * HD, D), (HEADS * HD) ** -0.5, 0.25),
        "covis": draw_covis(jax.random.fold_in(jax.random.fold_in(splits[6], part), 71), part),
        "block_view": jax.random.permutation(own_keys[5], NB).astype(jnp.int32),
    }


NEG = -1e30


def reference(queries, keys, values, out_weight, covis, block_view):
    vis = covis[block_view][:, block_view]
    scale = HD ** -0.5
    k3 = keys.astype(jnp.float32).reshape(TOKENS, HEADS, HD)
    v3 = values.astype(jnp.float32).reshape(TOKENS, HEADS, HD)
    q4 = queries.reshape(NB, BLOCK, HEADS, HD)

    def one_block(index):
        q = lax.dynamic_index_in_dim(q4, index, 0, keepdims=False).astype(jnp.float32)
        row = lax.dynamic_index_in_dim(vis, index, 0, keepdims=False)
        keep = (jnp.repeat(row, BLOCK) > 0)[None, None, :]
        scores = jnp.einsum("qhd,khd->qhk", q, k3) * scale
        scores = jnp.where(keep, scores, NEG)
        peak = jnp.max(scores, axis=-1, keepdims=True)
        probs = jnp.where(keep, jnp.exp(scores - peak), 0.0)
        total = jnp.sum(probs, axis=-1)
        rounded = lax.optimization_barrier(probs.astype(jnp.bfloat16))
        mixed = jnp.einsum("qhk,khd->qhd", rounded.astype(jnp.float32), v3) / total[..., None]
        return mixed.reshape(BLOCK, HEADS * HD).astype(jnp.bfloat16)

    attn = lax.map(one_block, jnp.arange(NB, dtype=jnp.int32)).reshape(TOKENS, HEADS * HD)
    return jnp.dot(attn, out_weight, preferred_element_type=jnp.float32).astype(jnp.bfloat16)
```

```python
import functools

import jax
import jax.numpy as jnp
from jax import lax
from jax.experimental import pallas as pl
from jax.experimental.pallas import tpu as pltpu
from jax.sharding import PartitionSpec as P

HEADS = 10
HD = 64
BLOCK = 32
PAIRS = HEADS // 2
LANES = 128
NEG = -1e30
MESH = pl.DeviceIdType.MESH
UP, DOWN, SIDE, CORE = 0, 1, 2, 3


def dot(a, b, ca, cb):
    return lax.dot_general(a, b, (((ca,), (cb,)), ((), ())), preferred_element_type=jnp.float32)


def iota(shape, dim):
    return lax.broadcasted_iota(jnp.int32, shape, dim)


def kernel(
    nz, ny, q_ref, k_ref, v_ref, w_ref, covis_ref, view_ref, o_ref,
    buf, qaug, acc, top, visq, send, recv, local,
):
    tok = q_ref.shape[0]
    per = tok // BLOCK
    count = covis_ref.shape[0]
    n_blk = nz * ny
    c = lax.axis_index("arc")
    b = lax.axis_index("blk")
    z = b // ny
    y = b % ny
    has_up = z < nz - 1
    has_down = z > 0
    mate = z + 1 - 2 * (z % 2)
    below, above = z, nz - 1 - z
    short = jnp.minimum(below, above)

    def order(i):
        step = (i + 1) // 2
        near = jnp.where(i % 2 == 1, z - step, z + step)
        far = jnp.where(above > below, z + (i - short), z - (i - short))
        return jnp.where(i <= 2 * short, near, far)

    def target(way):
        if way == UP:
            return {"blk": b + ny}
        if way == DOWN:
            return {"blk": b - ny}
        if way == SIDE:
            return {"blk": z * ny + (1 - y)}
        return {"arc": 1 - c}

    def place(piece, blk, core):
        return buf.at[piece, blk, pl.ds(pl.multiple_of(core * tok, 16), tok), :]

    def copy(way, piece, blk, src=None):
        dst = place(piece, blk, c)
        return pltpu.make_async_remote_copy(
            src_ref=dst if src is None else src,
            dst_ref=dst,
            send_sem=send.at[way, piece, blk],
            recv_sem=recv.at[piece, blk, c],
            device_id=target(way),
            device_id_type=MESH,
        )

    def arrive(piece, blk, core):
        dst = place(piece, blk, core)
        pltpu.make_async_remote_copy(
            src_ref=dst,
            dst_ref=dst,
            send_sem=send.at[CORE, piece, blk],
            recv_sem=recv.at[piece, blk, core],
            device_id=target(CORE),
            device_id_type=MESH,
        ).wait_recv()

    def along(piece, z0, act):
        blk = z0 * ny + y

        @pl.when((z0 <= z) & has_up)
        def _():
            act(copy(UP, piece, blk, None))

        @pl.when((z0 >= z) & has_down)
        def _():
            act(copy(DOWN, piece, blk, None))

        @pl.when(jnp.logical_or(piece == 0, z0 != mate))
        def _():
            act(copy(SIDE, piece, blk, None))

        act(copy(CORE, piece, blk, None))

    def across(piece, z0, act):
        blk = z0 * ny + (1 - y)
        if piece == 1:

            @pl.when((z0 == z) & (mate > z))
            def _():
                act(copy(UP, piece, blk))

            @pl.when((z0 == z) & (mate < z))
            def _():
                act(copy(DOWN, piece, blk))

        act(copy(CORE, piece, blk))

    def start(d):
        d.start()

    def done(d):
        d.wait_send()

    mine = [
        pltpu.make_async_copy(ref, place(piece, b, c), local.at[piece])
        for piece, ref in enumerate((k_ref, v_ref))
    ]
    for d in mine:
        d.start()

    barrier = pltpu.get_barrier_semaphore()

    @pl.when(has_up)
    def _():
        pl.semaphore_signal(barrier, inc=1, device_id=target(UP), device_id_type=MESH)

    @pl.when(has_down)
    def _():
        pl.semaphore_signal(barrier, inc=1, device_id=target(DOWN), device_id_type=MESH)

    pl.semaphore_signal(barrier, inc=1, device_id=target(SIDE), device_id_type=MESH)
    pl.semaphore_signal(barrier, inc=1, device_id=target(CORE), device_id_type=MESH)
    pl.semaphore_wait(barrier, 2 + has_up.astype(jnp.int32) + has_down.astype(jnp.int32))

    for piece in range(2):
        mine[piece].wait()
        along(piece, z, start)

    views = jnp.where(iota((count, count), 0) == view_ref[...], 1.0, 0.0).astype(jnp.bfloat16)
    seen = covis_ref[...].astype(jnp.float32).astype(jnp.bfloat16)
    half = dot(seen, views, 1, 0).astype(jnp.bfloat16)
    vis = dot(views, half, 0, 0).astype(jnp.bfloat16)
    first = (c * n_blk + b) * per
    own = (iota((count, LANES), 0) - first == iota((count, LANES), 1)) & (
        iota((count, LANES), 1) < per
    )
    visq[...] = dot(vis, jnp.where(own, 1.0, 0.0).astype(jnp.bfloat16), 0, 0).astype(jnp.bfloat16)

    left = iota((tok, LANES), 1) < HD
    onehot = jnp.where(iota((tok, LANES), 0) // BLOCK == iota((tok, LANES), 1), 1.0, 0.0)
    onehot = onehot.astype(jnp.bfloat16)
    for p in range(PAIRS):
        q = q_ref[:, p * LANES:(p + 1) * LANES].astype(jnp.float32) * HD ** (-0.5)
        qaug[p, :tok, :LANES] = jnp.where(left, q, 0.0).astype(jnp.bfloat16)
        qaug[p, tok:, :LANES] = jnp.where(left, 0.0, q).astype(jnp.bfloat16)
        qaug[p, :tok, LANES:] = onehot
        qaug[p, tok:, LANES:] = onehot
    acc[...] = jnp.zeros_like(acc)
    top[...] = jnp.full(top.shape, NEG, jnp.float32)

    def attend(blk):
        rows = 2 * tok
        r = iota((rows, count), 0)
        core = (r >= tok).astype(jnp.int32)
        slot = (core * n_blk + blk) * per + (r - core * tok) // BLOCK
        spread = jnp.where(slot == iota((rows, count), 1), 1.0, 0.0).astype(jnp.bfloat16)
        bias = ((1.0 - dot(spread, visq[...], 1, 0)) * NEG).astype(jnp.bfloat16)
        ones = jnp.ones((rows, LANES), jnp.bfloat16)
        for p in range(PAIRS):
            cols = slice(p * LANES, (p + 1) * LANES)
            keys = jnp.concatenate([buf[0, blk, :, cols], bias], axis=1)
            scores = dot(keys, qaug[p], 1, 1)
            before = top[p]
            fresh = jnp.maximum(before, jnp.max(scores, axis=0, keepdims=True))
            probs = jnp.exp(scores - fresh[:1]).astype(jnp.bfloat16)
            factor = jnp.exp(before - fresh)
            values = jnp.concatenate([buf[1, blk, :, cols], ones], axis=1)
            mixed = dot(values, probs, 0, 0)
            acc[p] = acc[p] * factor[:1] + mixed[:LANES + 8]
            top[p] = fresh

    def chunk(blk):
        arrive(0, blk, 1 - c)
        arrive(1, blk, 1 - c)
        attend(blk)

    chunk(b)

    def step(i, carry):
        z0, z1 = order(i), order(i - 1)
        for piece in range(2):
            arrive(piece, z0 * ny + y, c)
            along(piece, z0, start)
            arrive(piece, z1 * ny + (1 - y), c)
            across(piece, z1, start)
        chunk(z0 * ny + y)
        chunk(z1 * ny + (1 - y))
        return carry

    lax.fori_loop(1, nz, step, 0)
    last = order(nz - 1)
    for piece in range(2):
        arrive(piece, last * ny + (1 - y), c)
        across(piece, last, start)
    chunk(last * ny + (1 - y))

    parts = []
    for p in range(PAIRS):
        flat = (acc[p, :LANES] * (1.0 / acc[p, LANES:LANES + 1])).T
        parts.append(jnp.where(left, flat[:tok], flat[tok:]).astype(jnp.bfloat16))
    attn = jnp.concatenate(parts, axis=1)
    o_ref[...] = dot(attn, w_ref[...], 1, 0).astype(jnp.bfloat16)

    def drain(i, carry):
        for piece in range(2):
            along(piece, order(i), done)
            across(piece, order(i), done)
        return carry

    lax.fori_loop(0, nz, drain, 0)


def body(nz, ny, queries, keys, values, out_weight, covis, block_view):
    tok, width = queries.shape
    model = out_weight.shape[1]
    n_blk = nz * ny
    vmem = pl.BlockSpec(memory_space=pltpu.VMEM)
    hbm = pl.BlockSpec(memory_space=pl.ANY)
    return pl.pallas_call(
        functools.partial(kernel, nz, ny),
        out_shape=jax.ShapeDtypeStruct((tok, model), jnp.bfloat16),
        in_specs=[vmem, hbm, hbm, vmem, vmem, vmem],
        out_specs=vmem,
        scratch_shapes=[
            pltpu.VMEM((2, n_blk, 2 * tok, width), jnp.bfloat16),
            pltpu.VMEM((PAIRS, 2 * tok, 2 * LANES), jnp.bfloat16),
            pltpu.VMEM((PAIRS, LANES + 8, 2 * tok), jnp.float32),
            pltpu.VMEM((PAIRS, 8, 2 * tok), jnp.float32),
            pltpu.VMEM((covis.shape[0], LANES), jnp.bfloat16),
            pltpu.SemaphoreType.DMA((4, 2, n_blk)),
            pltpu.SemaphoreType.DMA((2, n_blk, 2)),
            pltpu.SemaphoreType.DMA((2,)),
        ],
        compiler_params=pltpu.CompilerParams(
            collective_id=0, has_side_effects=True, vmem_limit_bytes=56 * 2**20
        ),
    )(queries, keys, values, out_weight, covis, block_view[None, :])


def solution(mesh):
    ny = 2
    nz = mesh.shape["blk"] // ny
    return jax.shard_map(
        functools.partial(body, nz, ny),
        mesh=mesh,
        in_specs=(
            P(("groups", "arc", "blk"), None),
            P(("groups", "arc", "blk"), None),
            P(("groups", "arc", "blk"), None),
            P(),
            P("groups", None),
            P("groups"),
        ),
        out_specs=P(("groups", "arc", "blk"), None),
        check_vma=False,
    )
```

```python
import functools

import jax
import jax.numpy as jnp
from jax import lax
from jax.experimental import pallas as pl
from jax.experimental.pallas import tpu as pltpu
from jax.sharding import PartitionSpec as P

HEADS = 10
HD = 64
BLOCK = 32
PAIRS = HEADS // 2
LANES = 128
NEG = -1e30
MESH = pl.DeviceIdType.MESH
UP, DOWN, SIDE, CORE = 0, 1, 2, 3


def dot(a, b, ca, cb):
    return lax.dot_general(a, b, (((ca,), (cb,)), ((), ())), preferred_element_type=jnp.float32)


def iota(shape, dim):
    return lax.broadcasted_iota(jnp.int32, shape, dim)


def kernel(
    nz, ny, q_ref, k_ref, v_ref, covis_ref, view_ref, o_ref,
    buf, qaug, acc, top, visq, send, recv, local,
):
    tok = q_ref.shape[0]
    per = tok // BLOCK
    count = covis_ref.shape[0]
    n_blk = nz * ny
    c = lax.axis_index("arc")
    b = lax.axis_index("blk")
    z = b // ny
    y = b % ny
    has_up = z < nz - 1
    has_down = z > 0
    inner = has_up & has_down
    below, above = z, nz - 1 - z
    short = jnp.minimum(below, above)
    toward = jnp.where(below <= above, -1, 1)

    def order(i):
        step = (i + 1) // 2
        near = jnp.where(i % 2 == 1, z + toward * step, z - toward * step)
        far = z - toward * (i - short)
        return jnp.where(i <= 2 * short, near, far)

    def target(way):
        if way == UP:
            return {"blk": b + ny}
        if way == DOWN:
            return {"blk": b - ny}
        if way == SIDE:
            return {"blk": z * ny + (1 - y)}
        return {"arc": 1 - c}

    def place(piece, blk, core):
        return buf.at[piece, blk, pl.ds(pl.multiple_of(core * tok, 16), tok), :]

    def copy(way, piece, blk, src=None):
        dst = place(piece, blk, c)
        return pltpu.make_async_remote_copy(
            src_ref=dst if src is None else src,
            dst_ref=dst,
            send_sem=send.at[way, piece, blk],
            recv_sem=recv.at[piece, blk, c],
            device_id=target(way),
            device_id_type=MESH,
        )

    def arrive(piece, blk, core):
        dst = place(piece, blk, core)
        pltpu.make_async_remote_copy(
            src_ref=dst,
            dst_ref=dst,
            send_sem=send.at[CORE, piece, blk],
            recv_sem=recv.at[piece, blk, core],
            device_id=target(CORE),
            device_id_type=MESH,
        ).wait_recv()

    def along(piece, z0, act):
        blk = z0 * ny + y

        @pl.when((z0 <= z) & has_up)
        def _():
            act(copy(UP, piece, blk, None))

        @pl.when((z0 >= z) & has_down)
        def _():
            act(copy(DOWN, piece, blk, None))

        if piece == 0:
            act(copy(SIDE, piece, blk))
        else:

            @pl.when((z0 == z) | ((z0 > 0) & (z0 < nz - 1)))
            def _():
                act(copy(SIDE, piece, blk))

        act(copy(CORE, piece, blk, None))

    def across(piece, z0, act):
        blk = z0 * ny + (1 - y)
        if piece == 1:

            @pl.when((z0 == 0) & has_up)
            def _():
                act(copy(UP, piece, blk))

            @pl.when((z0 == nz - 1) & has_down)
            def _():
                act(copy(DOWN, piece, blk))

        act(copy(CORE, piece, blk))

    def start(d):
        d.start()

    def done(d):
        d.wait_send()

    mine = [
        pltpu.make_async_copy(ref, place(piece, b, c), local.at[piece])
        for piece, ref in enumerate((k_ref, v_ref))
    ]
    for d in mine:
        d.start()

    barrier = pltpu.get_barrier_semaphore()

    @pl.when(has_up)
    def _():
        pl.semaphore_signal(barrier, inc=1, device_id=target(UP), device_id_type=MESH)

    @pl.when(has_down)
    def _():
        pl.semaphore_signal(barrier, inc=1, device_id=target(DOWN), device_id_type=MESH)

    pl.semaphore_signal(barrier, inc=1, device_id=target(SIDE), device_id_type=MESH)
    pl.semaphore_signal(barrier, inc=1, device_id=target(CORE), device_id_type=MESH)
    pl.semaphore_wait(barrier, 2 + has_up.astype(jnp.int32) + has_down.astype(jnp.int32))

    for piece in range(2):
        mine[piece].wait()
        along(piece, z, start)

    views = jnp.where(iota((count, count), 0) == view_ref[...], 1.0, 0.0).astype(jnp.bfloat16)
    seen = covis_ref[...].astype(jnp.float32).astype(jnp.bfloat16)
    half = dot(seen, views, 1, 0).astype(jnp.bfloat16)
    vis = dot(views, half, 0, 0).astype(jnp.bfloat16)
    first = (c * n_blk + b) * per
    own = (iota((count, LANES), 0) - first == iota((count, LANES), 1)) & (
        iota((count, LANES), 1) < per
    )
    visq[...] = dot(vis, jnp.where(own, 1.0, 0.0).astype(jnp.bfloat16), 0, 0).astype(jnp.bfloat16)

    left = iota((tok, LANES), 1) < HD
    onehot = jnp.where(iota((tok, LANES), 0) // BLOCK == iota((tok, LANES), 1), 1.0, 0.0)
    onehot = onehot.astype(jnp.bfloat16)
    for p in range(PAIRS):
        q = q_ref[:, p * LANES:(p + 1) * LANES].astype(jnp.float32) * HD ** (-0.5)
        qaug[p, :tok, :LANES] = jnp.where(left, q, 0.0).astype(jnp.bfloat16)
        qaug[p, tok:, :LANES] = jnp.where(left, 0.0, q).astype(jnp.bfloat16)
        qaug[p, :tok, LANES:] = onehot
        qaug[p, tok:, LANES:] = onehot
    acc[...] = jnp.zeros_like(acc)
    top[...] = jnp.full(top.shape, NEG, jnp.float32)

    def attend(blk):
        rows = 2 * tok
        r = iota((rows, count), 0)
        core = (r >= tok).astype(jnp.int32)
        slot = (core * n_blk + blk) * per + (r - core * tok) // BLOCK
        spread = jnp.where(slot == iota((rows, count), 1), 1.0, 0.0).astype(jnp.bfloat16)
        bias = ((1.0 - dot(spread, visq[...], 1, 0)) * NEG).astype(jnp.bfloat16)
        ones = jnp.ones((rows, LANES), jnp.bfloat16)
        for p in range(PAIRS):
            cols = slice(p * LANES, (p + 1) * LANES)
            keys = jnp.concatenate([buf[0, blk, :, cols], bias], axis=1)
            scores = dot(keys, qaug[p], 1, 1)
            before = top[p]
            fresh = jnp.maximum(before, jnp.max(scores, axis=0, keepdims=True))
            probs = jnp.exp(scores - fresh[:1]).astype(jnp.bfloat16)
            factor = jnp.exp(before - fresh)
            values = jnp.concatenate([buf[1, blk, :, cols], ones], axis=1)
            mixed = dot(values, probs, 0, 0)
            acc[p] = acc[p] * factor[:1] + mixed[:LANES + 8]
            top[p] = fresh

    def chunk(blk):
        arrive(0, blk, 1 - c)
        arrive(1, blk, 1 - c)
        attend(blk)

    chunk(b)

    def near_events(i):
        for piece in range(2):
            arrive(piece, order(i) * ny + y, c)
            along(piece, order(i), start)

    def side_event(piece, i):
        arrive(piece, order(i) * ny + (1 - y), c)
        across(piece, order(i), start)

    def step(i, carry):
        near_events(i)
        side_event(0, i - 1)
        side_event(1, i - 1)
        chunk(order(i) * ny + y)
        chunk(order(i - 1) * ny + (1 - y))
        return carry

    lax.fori_loop(1, nz - 1, step, 0)
    last = nz - 1
    near_events(last)
    side_event(0, last - 1)
    side_event(1, last - 1)

    @pl.when(inner)
    def _():
        side_event(1, last)

    chunk(order(last) * ny + y)
    chunk(order(last - 1) * ny + (1 - y))
    side_event(0, last)

    @pl.when(jnp.logical_not(inner))
    def _():
        side_event(1, last)

    chunk(order(last) * ny + (1 - y))

    parts = []
    for p in range(PAIRS):
        flat = (acc[p, :LANES] * (1.0 / acc[p, LANES:LANES + 1])).T
        parts.append(jnp.where(left, flat[:tok], flat[tok:]).astype(jnp.bfloat16))
    o_ref[...] = jnp.concatenate(parts, axis=1)

    def drain(i, carry):
        for piece in range(2):
            along(piece, order(i), done)
            across(piece, order(i), done)
        return carry

    lax.fori_loop(0, nz, drain, 0)


def body(nz, ny, queries, keys, values, out_weight, covis, block_view):
    tok, width = queries.shape
    n_blk = nz * ny
    vmem = pl.BlockSpec(memory_space=pltpu.VMEM)
    hbm = pl.BlockSpec(memory_space=pl.ANY)
    attn = pl.pallas_call(
        functools.partial(kernel, nz, ny),
        out_shape=jax.ShapeDtypeStruct((tok, width), jnp.bfloat16),
        in_specs=[vmem, hbm, hbm, vmem, vmem],
        out_specs=vmem,
        scratch_shapes=[
            pltpu.VMEM((2, n_blk, 2 * tok, width), jnp.bfloat16),
            pltpu.VMEM((PAIRS, 2 * tok, 2 * LANES), jnp.bfloat16),
            pltpu.VMEM((PAIRS, LANES + 8, 2 * tok), jnp.float32),
            pltpu.VMEM((PAIRS, 8, 2 * tok), jnp.float32),
            pltpu.VMEM((covis.shape[0], LANES), jnp.bfloat16),
            pltpu.SemaphoreType.DMA((4, 2, n_blk)),
            pltpu.SemaphoreType.DMA((2, n_blk, 2)),
            pltpu.SemaphoreType.DMA((2,)),
        ],
        compiler_params=pltpu.CompilerParams(
            collective_id=0, has_side_effects=True, vmem_limit_bytes=56 * 2**20
        ),
    )(queries, keys, values, covis, block_view[None, :])
    return jnp.dot(attn, out_weight, preferred_element_type=jnp.float32).astype(jnp.bfloat16)


def solution(mesh):
    ny = 2
    nz = mesh.shape["blk"] // ny
    return jax.shard_map(
        functools.partial(body, nz, ny),
        mesh=mesh,
        in_specs=(
            P(("groups", "arc", "blk"), None),
            P(("groups", "arc", "blk"), None),
            P(("groups", "arc", "blk"), None),
            P(),
            P("groups", None),
            P("groups"),
        ),
        out_specs=P(("groups", "arc", "blk"), None),
        check_vma=False,
    )
```
